32 devices in a mesh: grp: 8 (over y, x, core), blk: 4 (over z).
Axes of the slice: x: 2, y: 2, z: 4, core: 2. Of those that a mesh axis runs over, the one named last changes fastest.
Arguments:
- targets: bfloat16 [4096, 128], P('blk'), may hold values from -6 to 6
- sources: bfloat16 [32768, 128], P(('grp', 'blk')), may hold values from -6 to 6
- panel: bfloat16 [32768, 32], P(('grp', 'blk')), may hold values from -6 to 6
Outputs:
- basis: float32 [4096, 32], P('blk')
The draws below stay inside these ranges and needn't reach their ends.
All inputs are finite; a program needn't handle non-finite values.
Results may differ from the reference program's by a relative error of at most 0.0003.
Values may be sent and summed in bfloat16 or wider, within the bound.
A program may use at most 64 MiB of HBM per device.

```python
import jax
import jax.numpy as jnp
from jax import lax

D = 128
K = 32
TGTS = 4096
SRCS = 32768


def block_levels(rng, shape, split, smallest, top_value):
    gain = 1.0
    for axis_at, parts in split:
        steps = jax.random.uniform(jax.random.fold_in(jax.random.fold_in(rng, 6), axis_at), (parts,), jnp.float32, smallest / len(split), top_value / len(split))
        gain = gain * jnp.repeat(jnp.exp(steps), shape[axis_at] // parts).reshape((-1,) + (1,) * (len(shape) - 1 - axis_at))
    return gain


def normal_values(stream_key, dims, spread, bound, shards=(), dtype=jnp.bfloat16):
    result = spread * jax.random.normal(stream_key, dims, jnp.float32)
    if shards:
        result = result * block_levels(stream_key, dims, shards, -0.22, 0.18)
    return jnp.clip(result, -bound, bound).astype(dtype)


def setup_inputs(seed: int = 0) -> dict:
    key_list = jax.random.split(jax.random.key(seed), 4)
    targets = normal_values(key_list[0], (TGTS, D), 1.0, 6.0, ((0, 4),))
    sources = normal_values(key_list[1], (SRCS, D), 1.0, 6.0, ((0, 32),))
    panel = normal_values(key_list[2], (SRCS, K), 1.0, 6.0, ((0, 32),))
    return {"targets": targets, "sources": sources, "panel": panel}


def block_product(tgt, src, pan):
    tgt_norm = jnp.sum(jnp.square(tgt.astype(jnp.float32)), axis=1)
    src_norm = jnp.sum(jnp.square(src.astype(jnp.float32)), axis=1)
    cross = jnp.dot(tgt.astype(jnp.float32), src.T.astype(jnp.float32), preferred_element_type=jnp.float32)
    dist = tgt_norm[:, None] + src_norm[None, :] - 2.0 * cross
    weight = jnp.exp(-(4.0 / D) * dist)
    return jnp.dot(weight, pan.astype(jnp.float32), precision=lax.Precision.HIGHEST)

def reference(targets, sources, panel):
    tgt_block = 1024 if TGTS % 1024 == 0 else TGTS
    src_block = 4096 if SRCS % 4096 == 0 else SRCS
    src_tiles = sources.reshape(SRCS // src_block, src_block, D)
    pan_tiles = panel.reshape(SRCS // src_block, src_block, K)

    def one_target_block(tgt):

        def step(total, pieces):
            return (total + block_product(tgt, pieces[0], pieces[1]), None)
        start = jnp.zeros((tgt.shape[0], K), jnp.float32)
        total, unused = lax.scan(step, start, (src_tiles, pan_tiles))
        return total
    product = lax.map(one_target_block, targets.reshape(TGTS // tgt_block, tgt_block, D))
    product = product.reshape(TGTS, K)
    gram = jnp.dot(product.T, product, precision=lax.Precision.HIGHEST) / TGTS
    lower = jnp.linalg.cholesky(gram)
    solved = jax.scipy.linalg.solve_triangular(lower, product.T, lower=True)
    return solved.T
```

```python
import functools

import jax
import jax.numpy as jnp
from jax import lax
from jax.experimental import pallas as pl
from jax.experimental.pallas import tpu as pltpu
from jax.sharding import PartitionSpec as P

D = 128
F32 = jnp.float32
BF16 = jnp.bfloat16
HIGHEST = lax.Precision.HIGHEST


def widened(rows, scale, first_own):
    full = rows.astype(F32)
    norm = jnp.sum(full * full, axis=1, keepdims=True) * (-4.0 / D)
    high = norm.astype(BF16).astype(F32)
    rest = norm - high
    mid = rest.astype(BF16).astype(F32)
    low = rest - mid
    lane = lax.broadcasted_iota(jnp.int32, full.shape, 1)
    own = 0 if first_own else 3
    extra = jnp.where(lane < 6, 1.0, 0.0)
    extra = jnp.where(lane == own, high, extra)
    extra = jnp.where(lane == own + 1, mid, extra)
    extra = jnp.where(lane == own + 2, low, extra)
    return jnp.concatenate([(full * scale).astype(BF16), extra.astype(BF16)], axis=1)


def inverse_lower(gram):
    k = gram.shape[0]
    row = lax.broadcasted_iota(jnp.int32, (k, k), 0)
    col = lax.broadcasted_iota(jnp.int32, (k, k), 1)
    left = gram
    right = jnp.where(row == col, 1.0, 0.0).astype(F32)
    for j in range(k - 1):
        inv = 1.0 / left[j : j + 1, j : j + 1]
        factor = jnp.where(row[:, 0:1] > j, left[:, j : j + 1] * inv, 0.0)
        right = right - factor * right[j : j + 1, :]
        left = left - factor * left[j : j + 1, :]
    pivots = jnp.sum(jnp.where(row == col, left, 0.0), axis=1, keepdims=True)
    return right / jnp.sqrt(pivots)


def kernel(
    grp, blk, total_rows,
    tgt, src, pan, out,
    saug, tall, part, rx_core, rx_chip, layer, rx_blk, full, grams,
    tz_s, tz_r, tl_s, tl_r, tc_s, tc_r,
    pc_s, pc_r, pq_s, pq_r, pb_s, pb_r, ag_s, ag_r, gr_s, gr_r,
):
    g = lax.axis_index("grp")
    b = lax.axis_index("blk")
    chips = grp // 2
    c = lax.rem(g, 2)
    q = g // 2
    piece = tgt.shape[0] // grp

    def send(source, dest, ssem, rsem, to_g, to_b):
        return pltpu.make_async_remote_copy(
            src_ref=source, dst_ref=dest, send_sem=ssem, recv_sem=rsem,
            device_id=(to_g, to_b), device_id_type=pl.DeviceIdType.MESH,
        )

    barrier = pltpu.get_barrier_semaphore()
    for f in range(1, grp):
        pl.semaphore_signal(barrier, inc=1, device_id=(lax.rem(g + f, grp), b), device_id_type=pl.DeviceIdType.MESH)
    for d in range(1, blk):
        pl.semaphore_signal(barrier, inc=1, device_id=(g, lax.rem(b + d, blk)), device_id_type=pl.DeviceIdType.MESH)
    pl.semaphore_wait(barrier, grp + blk - 2)

    sent = []

    def go(copy):
        copy.start()
        sent.append(copy)

    def up(d):
        return lax.rem(b + d, blk)

    def down(d):
        return lax.rem(b + blk - d, blk)

    def chip(e):
        return 2 * lax.rem(q + e, chips) + c

    def chip_back(e):
        return 2 * lax.rem(q + chips - e, chips) + c

    sib = 2 * q + 1 - c

    def tz(d):
        rows = tgt.at[pl.ds(pl.multiple_of(g * piece, piece), piece)]
        return send(rows, tall.at[b, g], tz_s.at[d - 1], tz_r.at[d - 1], g, up(d))

    def tl(d, e):
        return send(
            tall.at[down(d), g], tall.at[down(d), g],
            tl_s.at[d - 1, e - 1], tl_r.at[d - 1, e - 1], chip(e), b,
        )

    def tc(d, e):
        where = tall.at[down(d), chip_back(e)]
        return send(where, where, tc_s.at[d - 1, e], tc_r.at[d - 1, e], sib, b)

    for d in range(1, blk):
        go(tz(d))

    saug[...] = widened(src[...], 1.0, False)

    def product(rows):
        taug = widened(rows, 8.0 / D, True)
        power = lax.dot_general(taug, saug[...], (((1,), (1,)), ((), ())), preferred_element_type=F32)
        weight = jnp.exp(power)
        high = weight.astype(BF16)
        low = (weight - high.astype(F32)).astype(BF16)
        sums = jnp.dot(high, pan[...], preferred_element_type=F32)
        sums = sums + jnp.dot(low, pan[...], preferred_element_type=F32)
        return sums.T

    def own_chunks(lo, hi):
        def step(i, carry):
            rows = tgt[pl.ds(pl.multiple_of(i * piece, piece), piece)]
            part[b, lax.rem(i, 2), i // 2] = product(rows)
            return carry
        lax.fori_loop(lo, hi, step, 0)

    def other_chunks(d):
        bb = down(d)

        def step(i, carry):
            part[bb, lax.rem(i, 2), i // 2] = product(tall[bb, i])
            return carry
        lax.fori_loop(0, grp, step, 0)

    def pc(d):
        return send(part.at[down(d), 1 - c], rx_core.at[down(d)], pc_s.at[d], pc_r.at[d], sib, b)

    def pq(d, e):
        return send(
            part.at[down(d), c, lax.rem(q + e, chips)], rx_chip.at[down(d), e - 1],
            pq_s.at[d, e - 1], pq_r.at[d, e - 1], chip(e), b,
        )

    def pb(d):
        return send(layer.at[d], rx_blk.at[d - 1], pb_s.at[d - 1], pb_r.at[d - 1], g, down(d))

    def core_stage(d):
        bb = down(d)
        pc(d).wait_recv()
        part[bb, c] = part[bb, c] + rx_core[bb]
        for e in range(1, chips):
            go(pq(d, e))

    def chip_stage(d):
        bb = down(d)
        total = part[bb, c, q]
        for e in range(1, chips):
            pq(d, e).wait_recv()
            total = total + rx_chip[bb, e - 1]
        layer[d] = total
        if d > 0:
            go(pb(d))

    first, second = grp // 4, (grp * 5) // 8
    own_chunks(0, first)
    for d in range(1, blk):
        tz(d).wait_recv()
        go(tc(d, 0))
        for e in range(1, chips):
            go(tl(d, e))
    own_chunks(first, second)
    for d in range(1, blk):
        for e in range(1, chips):
            tl(d, e).wait_recv()
            go(tc(d, e))
    own_chunks(second, grp)
    go(pc(0))
    for d in range(1, blk):
        for e in range(chips):
            tc(d, e).wait_recv()
        other_chunks(d)
        go(pc(d))
        core_stage(d - 1)
        if d >= 2:
            chip_stage(d - 2)
    core_stage(blk - 1)
    if blk >= 2:
        chip_stage(blk - 2)
    chip_stage(blk - 1)
    mine = layer[0]
    for d in range(1, blk):
        pb(d).wait_recv()
        mine = mine + rx_blk[d - 1]
    full[g] = mine

    def ag(f):
        return send(full.at[g], full.at[g], ag_s.at[f - 1], ag_r.at[f - 1], lax.rem(g + f, grp), b)

    for f in range(1, grp):
        go(ag(f))
    for f in range(1, grp):
        ag(f).wait_recv()

    gram = jnp.zeros(grams.shape[1:], F32)
    for i in range(grp):
        gram = gram + lax.dot_general(
            full[i], full[i], (((1,), (1,)), ((), ())), precision=HIGHEST, preferred_element_type=F32
        )
    grams[b] = gram

    def gr(d):
        return send(grams.at[b], grams.at[b], gr_s.at[d - 1], gr_r.at[d - 1], g, up(d))

    for d in range(1, blk):
        go(gr(d))
    for d in range(1, blk):
        gr(d).wait_recv()
    gram = grams[0]
    for i in range(1, blk):
        gram = gram + grams[i]
    inverse = inverse_lower(gram * (1.0 / total_rows))
    for i in range(grp):
        out[:, i * piece : (i + 1) * piece] = jnp.dot(
            inverse, full[i], precision=HIGHEST, preferred_element_type=F32
        )
    for copy in sent:
        copy.wait_send()


def per_device(grp, blk, targets, sources, panel):
    rows, k = targets.shape[0], panel.shape[1]
    piece = rows // grp
    chips = grp // 2
    dma = lambda *shape: pltpu.SemaphoreType.DMA(shape)
    result = pl.pallas_call(
        functools.partial(kernel, grp, blk, rows * blk),
        out_shape=jax.ShapeDtypeStruct((k, rows), F32),
        in_specs=[pl.BlockSpec(memory_space=pltpu.VMEM)] * 3,
        out_specs=pl.BlockSpec(memory_space=pltpu.VMEM),
        scratch_shapes=[
            pltpu.VMEM((sources.shape[0], 2 * D), BF16),
            pltpu.VMEM((blk, grp, piece, D), BF16),
            pltpu.VMEM((blk, 2, chips, k, piece), F32),
            pltpu.VMEM((blk, chips, k, piece), F32),
            pltpu.VMEM((blk, chips - 1, k, piece), F32),
            pltpu.VMEM((blk, k, piece), F32),
            pltpu.VMEM((blk - 1, k, piece), F32),
            pltpu.VMEM((grp, k, piece), F32),
            pltpu.VMEM((blk, k, k), F32),
            dma(blk - 1), dma(blk - 1),
            dma(blk - 1, chips - 1), dma(blk - 1, chips - 1),
            dma(blk - 1, chips), dma(blk - 1, chips),
            dma(blk), dma(blk),
            dma(blk, chips - 1), dma(blk, chips - 1),
            dma(blk - 1), dma(blk - 1),
            dma(grp - 1), dma(grp - 1),
            dma(blk - 1), dma(blk - 1),
        ],
        compiler_params=pltpu.CompilerParams(
            collective_id=0, has_side_effects=True, vmem_limit_bytes=40 * 1024 * 1024
        ),
    )(targets, sources, panel)
    return result.T


def solution(mesh):
    in_specs = (P("blk", None), P(("grp", "blk"), None), P(("grp", "blk"), None))
    out_specs = P("blk", None)
    return jax.shard_map(
        functools.partial(per_device, mesh.shape["grp"], mesh.shape["blk"]),
        mesh=mesh, in_specs=in_specs, out_specs=out_specs, check_vma=False,
    )
```

```python
import functools

import jax
import jax.numpy as jnp
from jax import lax
from jax.experimental import pallas as pl
from jax.experimental.pallas import tpu as pltpu
from jax.sharding import PartitionSpec as P

D = 128
F32 = jnp.float32
BF16 = jnp.bfloat16
HIGHEST = lax.Precision.HIGHEST


def widened(rows, scale, first_own):
    full = rows.astype(F32)
    norm = jnp.sum(full * full, axis=1, keepdims=True) * (-4.0 / D)
    high = norm.astype(BF16).astype(F32)
    rest = norm - high
    mid = rest.astype(BF16).astype(F32)
    low = rest - mid
    lane = lax.broadcasted_iota(jnp.int32, full.shape, 1)
    own = 0 if first_own else 3
    extra = jnp.where(lane < 6, 1.0, 0.0)
    extra = jnp.where(lane == own, high, extra)
    extra = jnp.where(lane == own + 1, mid, extra)
    extra = jnp.where(lane == own + 2, low, extra)
    return jnp.concatenate([(full * scale).astype(BF16), extra.astype(BF16)], axis=1)


def inverse_lower(gram):
    k = gram.shape[0]
    row = lax.broadcasted_iota(jnp.int32, (k, k), 0)
    col = lax.broadcasted_iota(jnp.int32, (k, k), 1)
    left = gram
    right = jnp.where(row == col, 1.0, 0.0).astype(F32)
    for j in range(k - 1):
        inv = 1.0 / left[j : j + 1, j : j + 1]
        factor = jnp.where(row[:, 0:1] > j, left[:, j : j + 1] * inv, 0.0)
        right = right - factor * right[j : j + 1, :]
        left = left - factor * left[j : j + 1, :]
    pivots = jnp.sum(jnp.where(row == col, left, 0.0), axis=1, keepdims=True)
    return right / jnp.sqrt(pivots)


def kernel(
    grp, blk, total_rows,
    tgt_hbm, src_hbm, pan_hbm, out,
    src, pan, saug, tall, part, rx_rs, layer, rx_z, full,
    in_sem, tz_s, tz_r, tl_s, tl_r, tc_s, tc_r, rs_s, rs_r, zz_s, zz_r, ag_s, ag_r,
):
    g = lax.axis_index("grp")
    b = lax.axis_index("blk")
    chips = grp // 2
    c = lax.rem(g, 2)
    q = g // 2
    sib = 2 * q + 1 - c
    rows = tall.shape[1]
    piece = rows // grp
    k = pan.shape[0]

    def up(d):
        return lax.rem(b + d, blk)

    def down(d):
        return lax.rem(b + blk - d, blk)

    def peer(f):
        return lax.rem(g + f, grp)

    def chip(e):
        return 2 * lax.rem(q + e, chips) + c

    def chip_back(e):
        return 2 * lax.rem(q + chips - e, chips) + c

    def span(i):
        return pl.ds(pl.multiple_of(i * piece, piece), piece)

    barrier = pltpu.get_barrier_semaphore()
    for f in range(1, grp):
        pl.semaphore_signal(barrier, inc=1, device_id=(peer(f), b), device_id_type=pl.DeviceIdType.MESH)
    for d in range(1, blk):
        pl.semaphore_signal(barrier, inc=1, device_id=(g, up(d)), device_id_type=pl.DeviceIdType.MESH)
    load_src = pltpu.make_async_copy(src_hbm, src, in_sem.at[0])
    load_tgt = pltpu.make_async_copy(tgt_hbm, tall.at[b], in_sem.at[1])
    load_pan = pltpu.make_async_copy(pan_hbm, pan, in_sem.at[2])
    load_src.start()
    load_tgt.start()
    load_pan.start()

    def send(source, dest, ssem, rsem, to_g, to_b):
        return pltpu.make_async_remote_copy(
            src_ref=source, dst_ref=dest, send_sem=ssem, recv_sem=rsem,
            device_id=(to_g, to_b), device_id_type=pl.DeviceIdType.MESH,
        )

    def tz(d):
        return send(
            tgt_hbm.at[span(g)], tall.at[b, span(g)], tz_s.at[d - 1], tz_r.at[d - 1], g, up(d)
        )

    def tl(d, e):
        where = tall.at[down(d), span(g)]
        return send(where, where, tl_s.at[d - 1, e - 1], tl_r.at[d - 1, e - 1], chip(e), b)

    def tc(d, e):
        where = tall.at[down(d), span(chip_back(e))]
        return send(where, where, tc_s.at[d - 1, e], tc_r.at[d - 1, e], sib, b)

    def rs(d, f):
        return send(
            part.at[down(d), peer(f)], rx_rs.at[down(d), f - 1],
            rs_s.at[d, f - 1], rs_r.at[d, f - 1], peer(f), b,
        )

    def zz(i, h):
        return send(
            layer.at[i], rx_z.at[i, h - 1], zz_s.at[i, h - 1], zz_r.at[i, h - 1], g, up(h)
        )

    def ag(f):
        return send(full.at[g], full.at[g], ag_s.at[f - 1], ag_r.at[f - 1], peer(f), b)

    load_src.wait()
    saug[...] = widened(src[...], 1.0, False)
    pl.semaphore_wait(barrier, grp + blk - 2)
    for d in range(1, blk):
        tz(d).start()
    load_pan.wait()
    load_tgt.wait()

    def product(bb, start, count):
        taug = widened(tall[bb, start : start + count], 8.0 / D, True)
        step = min(saug.shape[0], 512)
        sums = jnp.zeros((k, count), F32)
        for lo in range(0, saug.shape[0], step):
            power = lax.dot_general(
                saug[lo : lo + step], taug, (((1,), (1,)), ((), ())), preferred_element_type=F32
            )
            weight = jnp.exp(power)
            high = weight.astype(BF16)
            low = (weight - high.astype(F32)).astype(BF16)
            sums = sums + jnp.dot(pan[:, lo : lo + step], high, preferred_element_type=F32)
            sums = sums + jnp.dot(pan[:, lo : lo + step], low, preferred_element_type=F32)
        for i in range(count // piece):
            part[bb, start // piece + i] = sums[:, i * piece : (i + 1) * piece]

    def layer_stage(d):
        i = down(d)
        total = part[i, g]
        for f in range(1, grp):
            rs(d, f).wait_recv()
            total = total + rx_rs[i, f - 1]
        layer[i] = total
        for h in range(1, blk):
            zz(i, h).start()

    product(b, 0, rows // 2)
    for d in range(1, blk):
        tz(d).wait_recv()
        for e in range(1, chips):
            tl(d, e).start()
        tc(d, 0).start()
    product(b, rows // 2, rows // 2)
    for f in range(1, grp):
        rs(0, f).start()
    for d in range(1, blk):
        for e in range(1, chips):
            tl(d, e).wait_recv()
            tc(d, e).start()

    def other(d, carry):
        for e in range(chips):
            tc(d, e).wait_recv()
        product(down(d), 0, rows)
        for f in range(1, grp):
            rs(d, f).start()
        layer_stage(d - 1)
        return carry

    lax.fori_loop(1, blk, other, 0)
    layer_stage(blk - 1)

    gram = jnp.zeros((k, k), F32)
    for i in range(blk):
        total = layer[i]
        for h in range(1, blk):
            zz(i, h).wait_recv()
            total = total + rx_z[i, h - 1]
        layer_done = total
        gram = gram + lax.dot_general(
            layer_done, layer_done, (((1,), (1,)), ((), ())),
            precision=HIGHEST, preferred_element_type=F32,
        )

        @pl.when(b == i)
        def _():
            full[g, 0:k] = layer_done

    if piece > k:
        gram = jnp.concatenate([gram, jnp.zeros((k, piece - k), F32)], axis=1)
    full[g, k : 2 * k] = gram
    for f in range(1, grp):
        ag(f).start()
    for f in range(1, grp):
        ag(f).wait_recv()
    gram = full[0, k : 2 * k, 0:k]
    for i in range(1, grp):
        gram = gram + full[i, k : 2 * k, 0:k]
    inverse = inverse_lower(gram * (1.0 / total_rows))
    for i in range(grp):
        out[:, i * piece : (i + 1) * piece] = jnp.dot(
            inverse, full[i, 0:k], precision=HIGHEST, preferred_element_type=F32
        )
    for d in range(1, blk):
        tz(d).wait_send()
        for e in range(chips):
            tc(d, e).wait_send()
        for e in range(1, chips):
            tl(d, e).wait_send()
    for d in range(blk):
        for f in range(1, grp):
            rs(d, f).wait_send()
        for h in range(1, blk):
            zz(d, h).wait_send()
    for f in range(1, grp):
        ag(f).wait_send()


def per_device(grp, blk, targets, sources, panel):
    rows, k = targets.shape[0], panel.shape[1]
    piece = rows // grp
    chips = grp // 2
    dma = lambda *shape: pltpu.SemaphoreType.DMA(shape)
    result = pl.pallas_call(
        functools.partial(kernel, grp, blk, rows * blk),
        out_shape=jax.ShapeDtypeStruct((k, rows), F32),
        in_specs=[pl.BlockSpec(memory_space=pltpu.HBM)] * 3,
        out_specs=pl.BlockSpec(memory_space=pltpu.VMEM),
        scratch_shapes=[
            pltpu.VMEM(sources.shape, BF16),
            pltpu.VMEM((k, sources.shape[0]), BF16),
            pltpu.VMEM((sources.shape[0], 2 * D), BF16),
            pltpu.VMEM((blk, rows, D), BF16),
            pltpu.VMEM((blk, grp, k, piece), F32),
            pltpu.VMEM((blk, grp - 1, k, piece), F32),
            pltpu.VMEM((blk, k, piece), F32),
            pltpu.VMEM((blk, blk - 1, k, piece), F32),
            pltpu.VMEM((grp, 2 * k, piece), F32),
            dma(3),
            dma(blk - 1), dma(blk - 1),
            dma(blk - 1, chips - 1), dma(blk - 1, chips - 1),
            dma(blk - 1, chips), dma(blk - 1, chips),
            dma(blk, grp - 1), dma(blk, grp - 1),
            dma(blk, blk - 1), dma(blk, blk - 1),
            dma(grp - 1), dma(grp - 1),
        ],
        compiler_params=pltpu.CompilerParams(
            collective_id=0, has_side_effects=True, vmem_limit_bytes=48 * 1024 * 1024
        ),
    )(targets, sources, panel.T)
    return result.T


def solution(mesh):
    in_specs = (P("blk", None), P(("grp", "blk"), None), P(("grp", "blk"), None))
    out_specs = P("blk", None)
    return jax.shard_map(
        functools.partial(per_device, mesh.shape["grp"], mesh.shape["blk"]),
        mesh=mesh, in_specs=in_specs, out_specs=out_specs, check_vma=False,
    )
```

```python
import functools

import jax
import jax.numpy as jnp
from jax import lax
from jax.experimental import pallas as pl
from jax.experimental.pallas import tpu as pltpu
from jax.sharding import PartitionSpec as P

D = 128
F32 = jnp.float32
BF16 = jnp.bfloat16
HIGHEST = lax.Precision.HIGHEST


def widened(rows, scale, first_own):
    full = rows.astype(F32)
    norm = jnp.sum(full * full, axis=1, keepdims=True) * (-4.0 / D)
    high = norm.astype(BF16).astype(F32)
    rest = norm - high
    mid = rest.astype(BF16).astype(F32)
    low = rest - mid
    lane = lax.broadcasted_iota(jnp.int32, full.shape, 1)
    own = 0 if first_own else 3
    extra = jnp.where(lane < 6, 1.0, 0.0)
    extra = jnp.where(lane == own, high, extra)
    extra = jnp.where(lane == own + 1, mid, extra)
    extra = jnp.where(lane == own + 2, low, extra)
    return jnp.concatenate([(full * scale).astype(BF16), extra.astype(BF16)], axis=1)


def inverse_lower(gram):
    k = gram.shape[0]
    row = lax.broadcasted_iota(jnp.int32, (k, k), 0)
    col = lax.broadcasted_iota(jnp.int32, (k, k), 1)
    left = gram
    right = jnp.where(row == col, 1.0, 0.0).astype(F32)
    for j in range(k - 1):
        inv = 1.0 / left[j : j + 1, j : j + 1]
        factor = jnp.where(row[:, 0:1] > j, left[:, j : j + 1] * inv, 0.0)
        right = right - factor * right[j : j + 1, :]
        left = left - factor * left[j : j + 1, :]
    pivots = jnp.sum(jnp.where(row == col, left, 0.0), axis=1, keepdims=True)
    return right / jnp.sqrt(pivots)


def kernel(
    grp, blk, total_rows,
    tgt_hbm, src_hbm, pan_hbm, out,
    src, pan, saug, tall, part, rx_rs, layer, rx_z, full,
    in_sem, tz_s, tz_r, tl_s, tl_r, tc_s, tc_r, rs_s, rs_r, zz_s, zz_r, ag_s, ag_r,
):
    g = lax.axis_index("grp")
    b = lax.axis_index("blk")
    chips = grp // 2
    c = lax.rem(g, 2)
    q = g // 2
    sib = 2 * q + 1 - c
    rows = tall.shape[1]
    piece = rows // grp
    k = pan.shape[0]

    def up(d):
        if blk & (blk - 1):
            return lax.rem(b + d, blk)
        bit, total = 1, 0
        while bit < blk:
            mine, flip = lax.rem(b // bit, 2), (d // bit) % 2
            total = total + bit * (mine + flip - 2 * mine * flip)
            bit *= 2
        return total

    def down(d):
        return lax.rem(b + blk - d, blk) if blk & (blk - 1) else up(d)

    def peer(f):
        return lax.rem(g + f, grp)

    def chip(e):
        return 2 * lax.rem(q + e, chips) + c

    def chip_back(e):
        return 2 * lax.rem(q + chips - e, chips) + c

    def span(i):
        return pl.ds(pl.multiple_of(i * piece, piece), piece)

    barrier = pltpu.get_barrier_semaphore()
    for f in range(1, grp):
        pl.semaphore_signal(barrier, inc=1, device_id=(peer(f), b), device_id_type=pl.DeviceIdType.MESH)
    for d in range(1, blk):
        pl.semaphore_signal(barrier, inc=1, device_id=(g, up(d)), device_id_type=pl.DeviceIdType.MESH)
    load_src = pltpu.make_async_copy(src_hbm, src, in_sem.at[0])
    load_tgt = pltpu.make_async_copy(tgt_hbm, tall.at[b], in_sem.at[1])
    load_pan = pltpu.make_async_copy(pan_hbm, pan, in_sem.at[2])
    load_src.start()
    load_tgt.start()
    load_pan.start()

    def send(source, dest, ssem, rsem, to_g, to_b):
        return pltpu.make_async_remote_copy(
            src_ref=source, dst_ref=dest, send_sem=ssem, recv_sem=rsem,
            device_id=(to_g, to_b), device_id_type=pl.DeviceIdType.MESH,
        )

    def tz(d):
        return send(
            tgt_hbm.at[span(g)], tall.at[b, span(g)], tz_s.at[d - 1], tz_r.at[d - 1], g, up(d)
        )

    def tl(d, e):
        where = tall.at[down(d), span(g)]
        return send(where, where, tl_s.at[d - 1, e - 1], tl_r.at[d - 1, e - 1], chip(e), b)

    def tc(d, e):
        where = tall.at[down(d), span(chip_back(e))]
        return send(where, where, tc_s.at[d - 1, e], tc_r.at[d - 1, e], sib, b)

    def rs(d, f):
        return send(
            part.at[down(d), peer(f)], rx_rs.at[down(d), f - 1],
            rs_s.at[d, f - 1], rs_r.at[d, f - 1], peer(f), b,
        )

    def zz(i, h):
        return send(
            layer.at[i], rx_z.at[i, h - 1], zz_s.at[i, h - 1], zz_r.at[i, h - 1], g, up(h)
        )

    def ag(f):
        return send(full.at[g], full.at[g], ag_s.at[f - 1], ag_r.at[f - 1], peer(f), b)

    load_src.wait()
    saug[...] = widened(src[...], 1.0, False)
    pl.semaphore_wait(barrier, grp + blk - 2)
    for d in range(1, blk):
        tz(d).start()
    load_pan.wait()
    load_tgt.wait()

    def product(bb, start, count):
        taug = widened(tall[bb, start : start + count], 8.0 / D, True)
        step = min(saug.shape[0], 512)
        sums = jnp.zeros((k, count), F32)
        for lo in range(0, saug.shape[0], step):
            power = lax.dot_general(
                saug[lo : lo + step], taug, (((1,), (1,)), ((), ())), preferred_element_type=F32
            )
            weight = jnp.exp(power)
            high = weight.astype(BF16)
            low = (weight - high.astype(F32)).astype(BF16)
            sums = sums + jnp.dot(pan[:, lo : lo + step], high, preferred_element_type=F32)
            sums = sums + jnp.dot(pan[:, lo : lo + step], low, preferred_element_type=F32)
        for i in range(count // piece):
            part[bb, start // piece + i] = sums[:, i * piece : (i + 1) * piece]

    def layer_stage(d):
        i = down(d)
        total = part[i, g]
        for f in range(1, grp):
            rs(d, f).wait_recv()
            total = total + rx_rs[i, f - 1]
        layer[i] = total
        for h in range(1, blk):
            zz(i, h).start()

    product(b, 0, rows // 2)
    for d in range(1, blk):
        tz(d).wait_recv()
        for e in range(1, chips):
            tl(d, e).start()
        tc(d, 0).start()
    product(b, rows // 2, rows // 2)
    for f in range(1, grp):
        rs(0, f).start()

    def forward(d):
        for e in range(1, chips):
            tl(d, e).wait_recv()
            tc(d, e).start()

    forward(1)

    def other(d, carry):
        for e in range(chips):
            tc(d, e).wait_recv()

        @pl.when(d < blk - 1)
        def _():
            forward(d + 1)

        product(down(d), 0, rows)
        for f in range(1, grp):
            rs(d, f).start()
        layer_stage(d - 1)
        return carry

    lax.fori_loop(1, blk, other, 0)
    layer_stage(blk - 1)

    gram = jnp.zeros((k, k), F32)
    for i in range(blk):
        total = layer[i]
        for h in range(1, blk):
            zz(i, h).wait_recv()
            total = total + rx_z[i, h - 1]
        layer_done = total
        gram = gram + lax.dot_general(
            layer_done, layer_done, (((1,), (1,)), ((), ())),
            precision=HIGHEST, preferred_element_type=F32,
        )

        @pl.when(b == i)
        def _():
            full[g, 0:k] = layer_done

    some = k * k // piece
    full[g, k : k + some] = jnp.concatenate(
        [gram[i * some : (i + 1) * some] for i in range(k // some)], axis=1
    )
    for f in range(1, grp):
        ag(f).start()
    for f in range(1, grp):
        ag(f).wait_recv()
    gram = full[0, k : k + some]
    for i in range(1, grp):
        gram = gram + full[i, k : k + some]
    gram = jnp.concatenate([gram[:, i * k : (i + 1) * k] for i in range(k // some)], axis=0)
    inverse = inverse_lower(gram * (1.0 / total_rows))
    for i in range(grp):
        out[:, i * piece : (i + 1) * piece] = jnp.dot(
            inverse, full[i, 0:k], precision=HIGHEST, preferred_element_type=F32
        )
    for d in range(1, blk):
        tz(d).wait_send()
        for e in range(chips):
            tc(d, e).wait_send()
        for e in range(1, chips):
            tl(d, e).wait_send()
    for d in range(blk):
        for f in range(1, grp):
            rs(d, f).wait_send()
        for h in range(1, blk):
            zz(d, h).wait_send()
    for f in range(1, grp):
        ag(f).wait_send()


def per_device(grp, blk, targets, sources, panel):
    rows, k = targets.shape[0], panel.shape[1]
    piece = rows // grp
    chips = grp // 2
    dma = lambda *shape: pltpu.SemaphoreType.DMA(shape)
    result = pl.pallas_call(
        functools.partial(kernel, grp, blk, rows * blk),
        out_shape=jax.ShapeDtypeStruct((k, rows), F32),
        in_specs=[pl.BlockSpec(memory_space=pltpu.HBM)] * 3,
        out_specs=pl.BlockSpec(memory_space=pltpu.VMEM),
        scratch_shapes=[
            pltpu.VMEM(sources.shape, BF16),
            pltpu.VMEM((k, sources.shape[0]), BF16),
            pltpu.VMEM((sources.shape[0], 2 * D), BF16),
            pltpu.VMEM((blk, rows, D), BF16),
            pltpu.VMEM((blk, grp, k, piece), F32),
            pltpu.VMEM((blk, grp - 1, k, piece), F32),
            pltpu.VMEM((blk, k, piece), F32),
            pltpu.VMEM((blk, blk - 1, k, piece), F32),
            pltpu.VMEM((grp, k + k * k // piece, piece), F32),
            dma(3),
            dma(blk - 1), dma(blk - 1),
            dma(blk - 1, chips - 1), dma(blk - 1, chips - 1),
            dma(blk - 1, chips), dma(blk - 1, chips),
            dma(blk, grp - 1), dma(blk, grp - 1),
            dma(blk, blk - 1), dma(blk, blk - 1),
            dma(grp - 1), dma(grp - 1),
        ],
        compiler_params=pltpu.CompilerParams(
            collective_id=0, has_side_effects=True, vmem_limit_bytes=64 * 1024 * 1024 - 65536
        ),
    )(targets, sources, panel.T)
    return result.T


def solution(mesh):
    in_specs = (P("blk", None), P(("grp", "blk"), None), P(("grp", "blk"), None))
    out_specs = P("blk", None)
    return jax.shard_map(
        functools.partial(per_device, mesh.shape["grp"], mesh.shape["blk"]),
        mesh=mesh, in_specs=in_specs, out_specs=out_specs, check_vma=False,
    )
```

```python
import functools
import math

import jax
import jax.numpy as jnp
from jax import lax
from jax.experimental import pallas as pl
from jax.experimental.pallas import tpu as pltpu
from jax.sharding import PartitionSpec as P

D = 128
F32 = jnp.float32
BF16 = jnp.bfloat16
HIGHEST = lax.Precision.HIGHEST


def widened(rows, scale, first_own):
    full = rows.astype(F32)
    norm = jnp.sum(full * full, axis=1, keepdims=True) * (-4.0 / D)
    high = norm.astype(BF16).astype(F32)
    rest = norm - high
    mid = rest.astype(BF16).astype(F32)
    low = rest - mid
    lane = lax.broadcasted_iota(jnp.int32, full.shape, 1)
    own = 0 if first_own else 3
    extra = jnp.where(lane < 6, 1.0, 0.0)
    extra = jnp.where(lane == own, high, extra)
    extra = jnp.where(lane == own + 1, mid, extra)
    extra = jnp.where(lane == own + 2, low, extra)
    return jnp.concatenate([(full * scale).astype(BF16), extra.astype(BF16)], axis=1)


def inverse_lower(gram):
    k = gram.shape[0]
    row = lax.broadcasted_iota(jnp.int32, (k, k), 0)
    col = lax.broadcasted_iota(jnp.int32, (k, k), 1)
    left = gram
    right = jnp.where(row == col, 1.0, 0.0).astype(F32)
    group = math.gcd(k, 8)
    for start in range(0, k, group):
        cols = [jnp.broadcast_to(left[:, j : j + 1], (k, k)) for j in range(start, start + group)]
        for m in range(group):
            j = start + m
            factor = jnp.where(row > j, cols[m] * (1.0 / cols[m][j : j + 1, :]), 0.0)
            right = right - factor * right[j : j + 1, :]
            left = left - factor * left[j : j + 1, :]
            for n in range(m + 1, group):
                cols[n] = cols[n] - factor * cols[n][j : j + 1, :]
    pivots = jnp.sum(jnp.where(row == col, left, 0.0), axis=1, keepdims=True)
    return right / jnp.sqrt(pivots)


def kernel(
    grp, blk, total_rows,
    tgt_hbm, src_hbm, pan_hbm, out,
    src, pan, saug, tall, part, rx_rs, layer, rx_z, full,
    in_sem, tz_s, tz_r, tl_s, tl_r, tc_s, tc_r, rs_s, rs_r, zz_s, zz_r, ag_s, ag_r,
):
    g = lax.axis_index("grp")
    b = lax.axis_index("blk")
    chips = grp // 2
    c = lax.rem(g, 2)
    q = g // 2
    sib = 2 * q + 1 - c
    rows = tall.shape[1]
    piece = rows // grp
    k = pan.shape[0]

    def up(d):
        if blk & (blk - 1):
            return lax.rem(b + d, blk)
        bit, total = 1, 0
        while bit < blk:
            mine, flip = lax.rem(b // bit, 2), (d // bit) % 2
            total = total + bit * (mine + flip - 2 * mine * flip)
            bit *= 2
        return total

    def down(d):
        return lax.rem(b + blk - d, blk) if blk & (blk - 1) else up(d)

    def peer(f):
        return lax.rem(g + f, grp)

    def chip(e):
        return 2 * lax.rem(q + e, chips) + c

    def chip_back(e):
        return 2 * lax.rem(q + chips - e, chips) + c

    def span(i):
        return pl.ds(pl.multiple_of(i * piece, piece), piece)

    barrier = pltpu.get_barrier_semaphore()
    for f in range(1, grp):
        pl.semaphore_signal(barrier, inc=1, device_id=(peer(f), b), device_id_type=pl.DeviceIdType.MESH)
    for d in range(1, blk):
        pl.semaphore_signal(barrier, inc=1, device_id=(g, up(d)), device_id_type=pl.DeviceIdType.MESH)
    load_src = pltpu.make_async_copy(src_hbm, src, in_sem.at[0])
    load_tgt = pltpu.make_async_copy(tgt_hbm, tall.at[b], in_sem.at[1])
    load_pan = pltpu.make_async_copy(pan_hbm, pan, in_sem.at[2])
    load_src.start()
    load_tgt.start()
    load_pan.start()

    def send(source, dest, ssem, rsem, to_g, to_b):
        return pltpu.make_async_remote_copy(
            src_ref=source, dst_ref=dest, send_sem=ssem, recv_sem=rsem,
            device_id=(to_g, to_b), device_id_type=pl.DeviceIdType.MESH,
        )

    def tz(d):
        return send(
            tgt_hbm.at[span(g)], tall.at[b, span(g)], tz_s.at[d - 1], tz_r.at[d - 1], g, up(d)
        )

    def tl(d, e):
        where = tall.at[down(d), span(g)]
        return send(where, where, tl_s.at[d - 1, e - 1], tl_r.at[d - 1, e - 1], chip(e), b)

    def tc(d, e):
        where = tall.at[down(d), span(chip_back(e))]
        return send(where, where, tc_s.at[d - 1, e], tc_r.at[d - 1, e], sib, b)

    def rs(d, f):
        return send(
            part.at[down(d), peer(f)], rx_rs.at[down(d), f - 1],
            rs_s.at[d, f - 1], rs_r.at[d, f - 1], peer(f), b,
        )

    def zz(i, h):
        return send(
            layer.at[i], rx_z.at[i, h - 1], zz_s.at[i, h - 1], zz_r.at[i, h - 1], g, up(h)
        )

    def ag(f):
        return send(full.at[g], full.at[g], ag_s.at[f - 1], ag_r.at[f - 1], peer(f), b)

    load_src.wait()
    saug[...] = widened(src[...], 1.0, False)
    pl.semaphore_wait(barrier, grp + blk - 2)
    for d in range(1, blk):
        tz(d).start()
    load_pan.wait()
    load_tgt.wait()

    def product(bb, start, count):
        taug = widened(tall[bb, start : start + count], 8.0 / D, True)
        step = min(saug.shape[0], 512)
        sums = jnp.zeros((k, count), F32)
        for lo in range(0, saug.shape[0], step):
            power = lax.dot_general(
                saug[lo : lo + step], taug, (((1,), (1,)), ((), ())), preferred_element_type=F32
            )
            weight = jnp.exp(power)
            high = weight.astype(BF16)
            low = (weight - high.astype(F32)).astype(BF16)
            sums = sums + jnp.dot(pan[:, lo : lo + step], high, preferred_element_type=F32)
            sums = sums + jnp.dot(pan[:, lo : lo + step], low, preferred_element_type=F32)
        for i in range(count // piece):
            part[bb, start // piece + i] = sums[:, i * piece : (i + 1) * piece]

    def layer_stage(d):
        i = down(d)
        total = part[i, g]
        for f in range(1, grp):
            rs(d, f).wait_recv()
            total = total + rx_rs[i, f - 1]
        layer[i] = total
        for h in range(1, blk):
            zz(i, h).start()

    def share(d):
        tz(d).wait_recv()
        for e in range(1, chips):
            tl(d, e).start()
        tc(d, 0).start()

    def forward(d):
        for e in range(1, chips):
            tl(d, e).wait_recv()
            tc(d, e).start()

    half = rows // 2
    share(1)
    product(b, 0, half)
    for d in range(2, min(blk, 3)):
        share(d)
    forward(1)
    product(b, half, half)
    for f in range(1, grp):
        rs(0, f).start()
    for d in range(3, blk):
        share(d)

    def other(d, carry):
        for e in range(chips):
            tc(d, e).wait_recv()

        @pl.when(d < blk - 1)
        def _():
            forward(d + 1)

        product(down(d), 0, rows)
        for f in range(1, grp):
            rs(d, f).start()
        layer_stage(d - 1)
        return carry

    lax.fori_loop(1, blk, other, 0)
    layer_stage(blk - 1)

    gram = jnp.zeros((k, k), F32)
    for i in range(blk):
        total = layer[i]
        for h in range(1, blk):
            zz(i, h).wait_recv()
            total = total + rx_z[i, h - 1]
        layer_done = total
        gram = gram + lax.dot_general(
            layer_done, layer_done, (((1,), (1,)), ((), ())),
            precision=HIGHEST, preferred_element_type=F32,
        )

        @pl.when(b == i)
        def _():
            full[g, 0:k] = layer_done

    some = k * k // piece
    full[g, k : k + some] = jnp.concatenate(
        [gram[i * some : (i + 1) * some] for i in range(k // some)], axis=1
    )
    for f in range(1, grp):
        ag(f).start()
    for f in range(1, grp):
        ag(f).wait_recv()
    gram = full[0, k : k + some]
    for i in range(1, grp):
        gram = gram + full[i, k : k + some]
    gram = jnp.concatenate([gram[:, i * k : (i + 1) * k] for i in range(k // some)], axis=0)
    inverse = inverse_lower(gram * (1.0 / total_rows))
    for i in range(grp):
        out[:, i * piece : (i + 1) * piece] = jnp.dot(
            inverse, full[i, 0:k], precision=HIGHEST, preferred_element_type=F32
        )
    for d in range(1, blk):
        tz(d).wait_send()
        for e in range(chips):
            tc(d, e).wait_send()
        for e in range(1, chips):
            tl(d, e).wait_send()
    for d in range(blk):
        for f in range(1, grp):
            rs(d, f).wait_send()
        for h in range(1, blk):
            zz(d, h).wait_send()
    for f in range(1, grp):
        ag(f).wait_send()


def per_device(grp, blk, targets, sources, panel):
    rows, k = targets.shape[0], panel.shape[1]
    piece = rows // grp
    chips = grp // 2
    dma = lambda *shape: pltpu.SemaphoreType.DMA(shape)
    result = pl.pallas_call(
        functools.partial(kernel, grp, blk, rows * blk),
        out_shape=jax.ShapeDtypeStruct((k, rows), F32),
        in_specs=[pl.BlockSpec(memory_space=pltpu.HBM)] * 3,
        out_specs=pl.BlockSpec(memory_space=pltpu.VMEM),
        scratch_shapes=[
            pltpu.VMEM(sources.shape, BF16),
            pltpu.VMEM((k, sources.shape[0]), BF16),
            pltpu.VMEM((sources.shape[0], 2 * D), BF16),
            pltpu.VMEM((blk, rows, D), BF16),
            pltpu.VMEM((blk, grp, k, piece), F32),
            pltpu.VMEM((blk, grp - 1, k, piece), F32),
            pltpu.VMEM((blk, k, piece), F32),
            pltpu.VMEM((blk, blk - 1, k, piece), F32),
            pltpu.VMEM((grp, k + k * k // piece, piece), F32),
            dma(3),
            dma(blk - 1), dma(blk - 1),
            dma(blk - 1, chips - 1), dma(blk - 1, chips - 1),
            dma(blk - 1, chips), dma(blk - 1, chips),
            dma(blk, grp - 1), dma(blk, grp - 1),
            dma(blk, blk - 1), dma(blk, blk - 1),
            dma(grp - 1), dma(grp - 1),
        ],
        compiler_params=pltpu.CompilerParams(
            collective_id=0, has_side_effects=True, vmem_limit_bytes=64 * 1024 * 1024 - 196608
        ),
    )(targets, sources, panel.T)
    return result.T


def solution(mesh):
    in_specs = (P("blk", None), P(("grp", "blk"), None), P(("grp", "blk"), None))
    out_specs = P("blk", None)
    return jax.shard_map(
        functools.partial(per_device, mesh.shape["grp"], mesh.shape["blk"]),
        mesh=mesh, in_specs=in_specs, out_specs=out_specs, check_vma=False,
    )
```

```python
import functools
import math

import jax
import jax.numpy as jnp
from jax import lax
from jax.experimental import pallas as pl
from jax.experimental.pallas import tpu as pltpu
from jax.sharding import PartitionSpec as P

D = 128
F32 = jnp.float32
BF16 = jnp.bfloat16
HIGHEST = lax.Precision.HIGHEST


def widened(rows, scale, first_own):
    full = rows.astype(F32)
    norm = jnp.sum(full * full, axis=1, keepdims=True) * (-4.0 / D)
    high = norm.astype(BF16).astype(F32)
    rest = norm - high
    mid = rest.astype(BF16).astype(F32)
    low = rest - mid
    lane = lax.broadcasted_iota(jnp.int32, full.shape, 1)
    own = 0 if first_own else 3
    extra = jnp.where(lane < 6, 1.0, 0.0)
    extra = jnp.where(lane == own, high, extra)
    extra = jnp.where(lane == own + 1, mid, extra)
    extra = jnp.where(lane == own + 2, low, extra)
    return jnp.concatenate([(full * scale).astype(BF16), extra.astype(BF16)], axis=1)


def inverse_lower(gram):
    k = gram.shape[0]
    row = lax.broadcasted_iota(jnp.int32, (k, k), 0)
    col = lax.broadcasted_iota(jnp.int32, (k, k), 1)
    left = gram
    right = jnp.where(row == col, 1.0, 0.0).astype(F32)
    group = math.gcd(k, 8)
    for start in range(0, k, group):
        cols = [jnp.broadcast_to(left[:, j : j + 1], (k, k)) for j in range(start, start + group)]
        for m in range(group):
            j = start + m
            factor = jnp.where(row > j, cols[m] * (1.0 / cols[m][j : j + 1, :]), 0.0)
            right = right - factor * right[j : j + 1, :]
            left = left - factor * left[j : j + 1, :]
            for n in range(m + 1, group):
                cols[n] = cols[n] - factor * cols[n][j : j + 1, :]
    pivots = jnp.sum(jnp.where(row == col, left, 0.0), axis=1, keepdims=True)
    return right / jnp.sqrt(pivots)


def kernel(
    grp, blk, total_rows,
    tgt_hbm, src_hbm, pan_hbm, out,
    src, pan, saug, tall, part, rx_rs, layer, rx_z, full,
    in_sem, tz_s, tz_r, tl_s, tl_r, tc_s, tc_r, rs_s, rs_r, zz_s, zz_r, ag_s, ag_r,
):
    g = lax.axis_index("grp")
    b = lax.axis_index("blk")
    chips = grp // 2
    c = lax.rem(g, 2)
    q = g // 2
    sib = 2 * q + 1 - c
    rows = tall.shape[1]
    piece = rows // grp
    k = pan.shape[0]

    def up(d):
        if blk & (blk - 1):
            return lax.rem(b + d, blk)
        bit, total = 1, 0
        while bit < blk:
            mine, flip = lax.rem(b // bit, 2), (d // bit) % 2
            total = total + bit * (mine + flip - 2 * mine * flip)
            bit *= 2
        return total

    def down(d):
        return lax.rem(b + blk - d, blk) if blk & (blk - 1) else up(d)

    def peer(f):
        return lax.rem(g + f, grp)

    def chip(e):
        return 2 * lax.rem(q + e, chips) + c

    def chip_back(e):
        return 2 * lax.rem(q + chips - e, chips) + c

    def span(i):
        return pl.ds(pl.multiple_of(i * piece, piece), piece)

    barrier = pltpu.get_barrier_semaphore()
    for f in range(1, grp):
        pl.semaphore_signal(barrier, inc=1, device_id=(peer(f), b), device_id_type=pl.DeviceIdType.MESH)
    for d in range(1, blk):
        pl.semaphore_signal(barrier, inc=1, device_id=(g, up(d)), device_id_type=pl.DeviceIdType.MESH)
    load_src = pltpu.make_async_copy(src_hbm, src, in_sem.at[0])
    load_tgt = pltpu.make_async_copy(tgt_hbm, tall.at[b], in_sem.at[1])
    load_pan = pltpu.make_async_copy(pan_hbm, pan, in_sem.at[2])
    load_src.start()
    load_tgt.start()
    load_pan.start()

    def send(source, dest, ssem, rsem, to_g, to_b):
        return pltpu.make_async_remote_copy(
            src_ref=source, dst_ref=dest, send_sem=ssem, recv_sem=rsem,
            device_id=(to_g, to_b), device_id_type=pl.DeviceIdType.MESH,
        )

    def tz(d):
        return send(
            tall.at[b, span(g)], tall.at[b, span(g)], tz_s.at[d - 1], tz_r.at[d - 1], g, up(d)
        )

    def tl(d, e):
        where = tall.at[down(d), span(g)]
        return send(where, where, tl_s.at[d - 1, e - 1], tl_r.at[d - 1, e - 1], chip(e), b)

    def tc(d, e):
        where = tall.at[down(d), span(chip_back(e))]
        return send(where, where, tc_s.at[d - 1, e], tc_r.at[d - 1, e], sib, b)

    def rs(d, f):
        return send(
            part.at[down(d), peer(f)], rx_rs.at[down(d), f - 1],
            rs_s.at[d, f - 1], rs_r.at[d, f - 1], peer(f), b,
        )

    def zz(i, h):
        return send(
            layer.at[i], rx_z.at[i, h - 1], zz_s.at[i, h - 1], zz_r.at[i, h - 1], g, up(h)
        )

    def ag(f):
        return send(full.at[g], full.at[g], ag_s.at[f - 1], ag_r.at[f - 1], peer(f), b)

    load_src.wait()
    saug[...] = widened(src[...], 1.0, False)
    load_tgt.wait()
    load_pan.wait()
    pl.semaphore_wait(barrier, grp + blk - 2)
    for d in range(1, blk):
        tz(d).start()

    def product(bb, start, count):
        taug = widened(tall[bb, start : start + count], 8.0 / D, True)
        step = min(saug.shape[0], 512)
        sums = jnp.zeros((k, count), F32)
        for lo in range(0, saug.shape[0], step):
            power = lax.dot_general(
                saug[lo : lo + step], taug, (((1,), (1,)), ((), ())), preferred_element_type=F32
            )
            weight = jnp.exp(power)
            high = weight.astype(BF16)
            low = (weight - high.astype(F32)).astype(BF16)
            sums = sums + jnp.dot(pan[:, lo : lo + step], high, preferred_element_type=F32)
            sums = sums + jnp.dot(pan[:, lo : lo + step], low, preferred_element_type=F32)
        for i in range(count // piece):
            part[bb, start // piece + i] = sums[:, i * piece : (i + 1) * piece]

    def layer_stage(d):
        i = down(d)
        total = part[i, g]
        for f in range(1, grp):
            rs(d, f).wait_recv()
            total = total + rx_rs[i, f - 1]
        layer[i] = total
        for h in range(1, blk):
            zz(i, h).start()

    def share(d):
        tz(d).wait_recv()
        for e in range(1, chips):
            tl(d, e).start()
        tc(d, 0).start()

    def forward(d):
        for e in range(1, chips):
            tl(d, e).wait_recv()
            tc(d, e).start()

    half = rows // 2
    share(1)
    product(b, 0, half)
    for d in range(2, min(blk, 3)):
        share(d)
    forward(1)
    product(b, half, half)
    for f in range(1, grp):
        rs(0, f).start()
    for d in range(3, blk):
        share(d)

    def other(d, carry):
        for e in range(chips):
            tc(d, e).wait_recv()

        @pl.when(d < blk - 1)
        def _():
            forward(d + 1)

        product(down(d), 0, rows)
        for f in range(1, grp):
            rs(d, f).start()
        layer_stage(d - 1)
        return carry

    lax.fori_loop(1, blk, other, 0)
    layer_stage(blk - 1)

    gram = jnp.zeros((k, k), F32)
    for i in range(blk):
        total = layer[i]
        for h in range(1, blk):
            zz(i, h).wait_recv()
            total = total + rx_z[i, h - 1]
        layer_done = total
        gram = gram + lax.dot_general(
            layer_done, layer_done, (((1,), (1,)), ((), ())),
            precision=HIGHEST, preferred_element_type=F32,
        )

        @pl.when(b == i)
        def _():
            full[g, 0:k] = layer_done

    some = k * k // piece
    full[g, k : k + some] = jnp.concatenate(
        [gram[i * some : (i + 1) * some] for i in range(k // some)], axis=1
    )
    for f in range(1, grp):
        ag(f).start()
    for f in range(1, grp):
        ag(f).wait_recv()
    gram = full[0, k : k + some]
    for i in range(1, grp):
        gram = gram + full[i, k : k + some]
    gram = jnp.concatenate([gram[:, i * k : (i + 1) * k] for i in range(k // some)], axis=0)
    inverse = inverse_lower(gram * (1.0 / total_rows))
    for i in range(grp):
        out[:, i * piece : (i + 1) * piece] = jnp.dot(
            inverse, full[i, 0:k], precision=HIGHEST, preferred_element_type=F32
        )
    for d in range(1, blk):
        tz(d).wait_send()
        for e in range(chips):
            tc(d, e).wait_send()
        for e in range(1, chips):
            tl(d, e).wait_send()
    for d in range(blk):
        for f in range(1, grp):
            rs(d, f).wait_send()
        for h in range(1, blk):
            zz(d, h).wait_send()
    for f in range(1, grp):
        ag(f).wait_send()


def per_device(grp, blk, targets, sources, panel):
    rows, k = targets.shape[0], panel.shape[1]
    piece = rows // grp
    chips = grp // 2
    dma = lambda *shape: pltpu.SemaphoreType.DMA(shape)
    result = pl.pallas_call(
        functools.partial(kernel, grp, blk, rows * blk),
        out_shape=jax.ShapeDtypeStruct((k, rows), F32),
        in_specs=[pl.BlockSpec(memory_space=pltpu.HBM)] * 3,
        out_specs=pl.BlockSpec(memory_space=pltpu.VMEM),
        scratch_shapes=[
            pltpu.VMEM(sources.shape, BF16),
            pltpu.VMEM((k, sources.shape[0]), BF16),
            pltpu.VMEM((sources.shape[0], 2 * D), BF16),
            pltpu.VMEM((blk, rows, D), BF16),
            pltpu.VMEM((blk, grp, k, piece), F32),
            pltpu.VMEM((blk, grp - 1, k, piece), F32),
            pltpu.VMEM((blk, k, piece), F32),
            pltpu.VMEM((blk, blk - 1, k, piece), F32),
            pltpu.VMEM((grp, k + k * k // piece, piece), F32),
            dma(3),
            dma(blk - 1), dma(blk - 1),
            dma(blk - 1, chips - 1), dma(blk - 1, chips - 1),
            dma(blk - 1, chips), dma(blk - 1, chips),
            dma(blk, grp - 1), dma(blk, grp - 1),
            dma(blk, blk - 1), dma(blk, blk - 1),
            dma(grp - 1), dma(grp - 1),
        ],
        compiler_params=pltpu.CompilerParams(
            collective_id=0, has_side_effects=True, vmem_limit_bytes=48 * 1024 * 1024
        ),
    )(*[pltpu.with_memory_space_constraint(x, pltpu.HBM) for x in (targets, sources, panel.T)])
    return result.T


def solution(mesh):
    in_specs = (P("blk", None), P(("grp", "blk"), None), P(("grp", "blk"), None))
    out_specs = P("blk", None)
    return jax.shard_map(
        functools.partial(per_device, mesh.shape["grp"], mesh.shape["blk"]),
        mesh=mesh, in_specs=in_specs, out_specs=out_specs, check_vma=False,
    )
```
